32 devices in a mesh: sa: 4 (over y, x), sb: 8 (over z, core).
Axes of the slice: x: 2, y: 2, z: 4, core: 2. Of those that a mesh axis runs over, the one named last changes fastest.
Arguments:
- tokens: bfloat16 [16, 32, 128, 768], P('sa', 'sb'), may hold values from -6 to 6
- cotangent: bfloat16 [16, 32, 128, 768], P('sa', 'sb'), may hold values from -6 to 6
- in_weight: bfloat16 [768, 1536], replicated, may hold values from -0.21875 to 0.21875
- out_weight: bfloat16 [768, 768], replicated, may hold values from -0.21875 to 0.21875
- factor_c: bfloat16 [16, 128, 128], P('sa'), may hold values from -0.5 to 0.5
- factor_a: bfloat16 [32, 16, 16], P('sb'), may hold values from -1.5 to 1.5
- factor_b: bfloat16 [128, 32, 32], P(('sa', 'sb')), may hold values from -1 to 1
Outputs:
- grad_tokens: bfloat16 [16, 32, 128, 768], P('sa', 'sb')
- grad_in_weight: float32 [768, 1536], replicated
- grad_out_weight: float32 [768, 768], replicated
- grad_factor_c: float32 [16, 128, 128], P('sa')
- grad_factor_a: float32 [32, 16, 16], P('sb')
- grad_factor_b: float32 [128, 32, 32], P(('sa', 'sb'))
The draws below stay inside these ranges and needn't reach their ends.
All inputs are finite; a program needn't handle non-finite values.
Results may differ from the reference program's by a relative error of at most 0.0087.
Values may be sent and summed in bfloat16 or wider, within the bound.
A program may use at most 128 MiB of HBM per device.

```python
import math
import jax
import jax.numpy as jnp
from jax import lax

D = 768
C = 128
A = 16
B = 32
TOKENS = 65536


def levels(key, dims, cuts, least, largest):
    level, own = 1.0, jax.random.fold_in(key, 6)
    for position, parts in cuts:
        steps = jnp.exp(jax.random.uniform(jax.random.fold_in(own, position), (parts,), jnp.float32, least / len(cuts), largest / len(cuts)))
        level = level * jnp.repeat(steps, dims[position] // parts).reshape([-1 if axis == position else 1 for axis in range(len(dims))])
    return level


def scatter_about(rng, extent, width, limit, cuts=(), dtype=jnp.bfloat16):
    values = width * jax.random.normal(rng, extent, jnp.float32)
    if cuts:
        values = values * levels(rng, extent, cuts, -0.22, 0.18)
    return jnp.clip(values, -limit, limit).astype(dtype)


def setup_inputs(seed: int = 0) -> dict:
    key_of = jax.random.split(jax.random.key(seed), 8)
    tokens = scatter_about(key_of[0], (A, B, C, D), 1.0, 6.0, ((0, 4), (1, 8)))
    cotangent = scatter_about(key_of[1], (A, B, C, D), 1.0, 6.0, ((0, 4), (1, 8)))
    in_weight = scatter_about(key_of[2], (D, 2 * D), D ** -0.5, 0.21875)
    out_weight = scatter_about(key_of[3], (D, D), D ** -0.5, 0.21875)
    factor_c = scatter_about(key_of[4], (A, C, C), C ** -0.5, 0.5, ((0, 4),))
    factor_a = scatter_about(key_of[5], (B, A, A), A ** -0.5, 1.5, ((0, 8),))
    factor_b = scatter_about(key_of[6], (C, B, B), B ** -0.5, 1.0, ((0, 32),))
    return {"tokens": tokens, "cotangent": cotangent, "in_weight": in_weight, "out_weight": out_weight, "factor_c": factor_c, "factor_a": factor_a, "factor_b": factor_b}


def levels_forward(values, factor_c, factor_a, factor_b):
    section_one = jnp.einsum('akc,abcd->abkd', factor_c, values.astype(jnp.float32)).astype(jnp.bfloat16)
    section_two = jnp.einsum('bka,abcd->kbcd', factor_a, section_one.astype(jnp.float32)).astype(jnp.bfloat16)
    mixing = jnp.einsum('ckb,abcd->akcd', factor_b, section_two.astype(jnp.float32)).astype(jnp.bfloat16)
    return (section_one, section_two, mixing)

def reference(tokens, cotangent, in_weight, out_weight, factor_c, factor_a, factor_b):
    block_size = 128 if D % 128 == 0 else D
    block_count = D // block_size
    wide_c = factor_c.astype(jnp.float32)
    wide_a = factor_a.astype(jnp.float32)
    wide_b = factor_b.astype(jnp.float32)
    scale = 1.0 / math.sqrt(TOKENS)

    def project(row_block):
        projected = jnp.dot(row_block.reshape(B * C, D), in_weight, preferred_element_type=jnp.float32)
        queries = projected[:, :D].astype(jnp.bfloat16).reshape(B, C, D)
        values = projected[:, D:].astype(jnp.bfloat16).reshape(B, C, D)
        return (queries, values)
    queries, values = lax.map(project, tokens)

    def split_channels(tensor):
        return jnp.moveaxis(tensor.reshape(A, B, C, block_count, block_size), 3, 0)

    def join_channels(tensor):
        return jnp.moveaxis(tensor, 0, 3).reshape(A, B, C, D)

    def mix_block(value_block):
        return levels_forward(value_block, wide_c, wide_a, wide_b)[2]
    mixing = join_channels(lax.map(mix_block, split_channels(values)))

    def gate_step(totals, pieces):
        query_rows, mixing_rows, cot_rows = pieces
        query_wide = query_rows.reshape(B * C, D).astype(jnp.float32)
        mixing_wide = mixing_rows.reshape(B * C, D).astype(jnp.float32)
        cot_flat = cot_rows.reshape(B * C, D)
        sigmoid_q = jax.nn.sigmoid(query_wide)
        activation = query_wide * sigmoid_q
        slope = sigmoid_q * (1.0 + query_wide * (1.0 - sigmoid_q))
        gated = (activation * mixing_wide).astype(jnp.bfloat16)
        grad_gated = lax.dot_general(cot_flat, out_weight, (((1,), (1,)), ((), ())), preferred_element_type=jnp.float32)
        totals = totals + lax.dot_general(gated, cot_flat, (((0,), (0,)), ((), ())), preferred_element_type=jnp.float32)
        grad_mixing = (grad_gated * activation).astype(jnp.bfloat16).reshape(B, C, D)
        grad_queries = (grad_gated * mixing_wide * slope).astype(jnp.bfloat16).reshape(B, C, D)
        return (totals, (grad_mixing, grad_queries))
    out_totals, (grad_mixing, grad_queries) = lax.scan(gate_step, jnp.zeros((D, D), jnp.float32), (queries, mixing, cotangent))

    def back_step(totals, pieces):
        value_block, grad_block = pieces
        section_one, section_two, unused = levels_forward(value_block, wide_c, wide_a, wide_b)
        grad_wide = grad_block.astype(jnp.float32)
        grad_two = jnp.einsum('ckb,akcd->abcd', wide_b, grad_wide).astype(jnp.bfloat16)
        grad_one = jnp.einsum('bka,kbcd->abcd', wide_a, grad_two.astype(jnp.float32)).astype(jnp.bfloat16)
        grad_values = jnp.einsum('akc,abkd->abcd', wide_c, grad_one.astype(jnp.float32)).astype(jnp.bfloat16)
        term_b = jnp.einsum('akcd,abcd->ckb', grad_wide, section_two.astype(jnp.float32))
        term_a = jnp.einsum('kbcd,abcd->bka', grad_two.astype(jnp.float32), section_one.astype(jnp.float32))
        term_c = jnp.einsum('abkd,abcd->akc', grad_one.astype(jnp.float32), value_block.astype(jnp.float32))
        return ((totals[0] + term_c, totals[1] + term_a, totals[2] + term_b), grad_values)
    start = (jnp.zeros((A, C, C), jnp.float32), jnp.zeros((B, A, A), jnp.float32), jnp.zeros((C, B, B), jnp.float32))
    factor_totals, grad_value_blocks = lax.scan(back_step, start, (split_channels(values), split_channels(grad_mixing)))
    grad_values = join_channels(grad_value_blocks)

    def tail_step(totals, pieces):
        token_rows, query_rows, value_rows = pieces
        grad_projected = jnp.concatenate([query_rows.reshape(B * C, D), value_rows.reshape(B * C, D)], axis=1)
        grad_rows = lax.dot_general(grad_projected, in_weight, (((1,), (1,)), ((), ())), preferred_element_type=jnp.float32)
        totals = totals + lax.dot_general(token_rows.reshape(B * C, D), grad_projected, (((0,), (0,)), ((), ())), preferred_element_type=jnp.float32)
        return (totals, grad_rows.astype(jnp.bfloat16).reshape(B, C, D))
    in_totals, grad_tokens = lax.scan(tail_step, jnp.zeros((D, 2 * D), jnp.float32), (tokens, grad_queries, grad_values))
    return (grad_tokens, in_totals * scale, out_totals * scale, factor_totals[0] * scale, factor_totals[1] * scale, factor_totals[2] * scale)
```

```python
import functools
import math

import jax
import jax.numpy as jnp
from jax import lax
from jax.experimental import pallas as pl
from jax.experimental.pallas import tpu as pltpu
from jax.sharding import PartitionSpec as P

CONTRACT_ROWS = (((0,), (0,)), ((), ()))
CONTRACT_COLUMNS = (((1,), (1,)), ((), ()))
S1, B1, B2, S2, S3, B3, B4, S4 = range(8)


def product_rows(left, right):
    return lax.dot_general(left, right, CONTRACT_ROWS, preferred_element_type=jnp.float32)


def product_columns(left, right):
    return lax.dot_general(left, right, CONTRACT_COLUMNS, preferred_element_type=jnp.float32)


def product(left, right):
    return jnp.dot(left, right, preferred_element_type=jnp.float32)


def mixer_kernel(
    dims,
    v_ref, g_ref, fc_ref, perm_ref, ma_ref, mb_ref,
    mix_ref, gv_ref, gfc_ref, gfa_ref, gfb_ref,
    send1, send2, send3, og, ig, mo, mi, go, gi, g2o, g1t,
    send_sem, recv_sem,
):
    na, nb, a_dev, b_dev, positions, rows_c, group, rows_b, width, chunks = dims
    block = a_dev * rows_c
    outer_rows = na * block
    me_a = lax.axis_index("sa")
    me_b = lax.axis_index("sb")
    bf16 = jnp.bfloat16

    def peer_a(t):
        return lax.rem(me_a + t, na)

    def peer_b(t):
        return lax.rem(me_b + t, nb)

    barrier = pltpu.get_barrier_semaphore()

    def greet_a(t, carry):
        pl.semaphore_signal(barrier, inc=1, device_id={"sa": peer_a(t)}, device_id_type=pl.DeviceIdType.MESH)
        return carry

    def greet_b(t, carry):
        pl.semaphore_signal(barrier, inc=1, device_id={"sb": peer_b(t)}, device_id_type=pl.DeviceIdType.MESH)
        return carry

    lax.fori_loop(1, na, greet_a, 0)
    lax.fori_loop(1, nb, greet_b, 0)
    pl.semaphore_wait(barrier, na + nb - 2)

    gfc_ref[...] = jnp.zeros_like(gfc_ref)
    gfa_ref[...] = jnp.zeros_like(gfa_ref)
    gfb_ref[...] = jnp.zeros_like(gfb_ref)

    def scatter_copy(op, q, src, dst, peer, slot):
        return pltpu.make_async_remote_copy(
            src_ref=src.at[q, peer],
            dst_ref=dst.at[q, :, slot],
            send_sem=send_sem.at[op, q, peer],
            recv_sem=recv_sem.at[op, q, slot],
            device_id={"sa": peer},
            device_id_type=pl.DeviceIdType.MESH,
        )

    def collect_copy(op, q, src, dst, peer, slot):
        return pltpu.make_async_remote_copy(
            src_ref=src.at[q, :, peer],
            dst_ref=dst.at[q, slot],
            send_sem=send_sem.at[op, q, peer],
            recv_sem=recv_sem.at[op, q, slot],
            device_id={"sa": peer},
            device_id_type=pl.DeviceIdType.MESH,
        )

    def middle_copy(op, q, src, dst, peer, slot):
        return pltpu.make_async_remote_copy(
            src_ref=src.at[q, :, peer] if op in (B2, B4) else src.at[q, peer],
            dst_ref=dst.at[q, slot],
            send_sem=send_sem.at[op, q, peer],
            recv_sem=recv_sem.at[op, q, slot],
            device_id={"sb": peer},
            device_id_type=pl.DeviceIdType.MESH,
        )

    plan = {
        S1: (scatter_copy, send1, og),
        S2: (collect_copy, mo, mi),
        S3: (scatter_copy, send3, go),
        S4: (collect_copy, send2, g1t),
        B1: (middle_copy, send2, ig),
        B2: (middle_copy, send1, mo),
        B3: (middle_copy, go, gi),
        B4: (middle_copy, send3, g2o),
    }

    def start(op, q):
        make, src, dst = plan[op]
        over_b = make is middle_copy
        me, size, peer_of = (me_b, nb, peer_b) if over_b else (me_a, na, peer_a)

        def one(t, carry):
            make(op, q, src, dst, peer_of(t), me).start()
            return carry

        lax.fori_loop(1, size, one, 0)
        if make is scatter_copy:
            dst[q, :, me] = src[q, me]
        elif op in (B1, B3):
            dst[q, me] = src[q, me]
        else:
            dst[q, me] = src[q, :, me]

    def wait(op, q, sends):
        make, src, dst = plan[op]
        size, peer_of = (nb, peer_b) if make is middle_copy else (na, peer_a)

        def one(t, carry):
            peer = peer_of(t)
            copy = make(op, q, src, dst, peer, peer)
            if sends:
                copy.wait_send()
            else:
                copy.wait_recv()
            return carry

        lax.fori_loop(1, size, one, 0)

    pairs = group * b_dev
    span = pairs * positions
    steps_c = a_dev // group
    slab = group * rows_c

    def columns(q):
        return slice(q * width, (q + 1) * width)

    def native(s, p):
        return pl.ds(pl.multiple_of(s * span + p * positions, 128), positions)

    def slab_rows(s):
        return pl.ds(pl.multiple_of(s * slab, 16), slab)

    def spread(value, dst, q, s):
        moved = product(perm_ref[...], value).astype(bf16)
        dst[q, :, :, slab_rows(s), :] = moved.reshape(na, nb, slab, width)

    def unspread(src, q, s):
        value = src[q, :, :, slab_rows(s), :].reshape(span, width)
        return product_rows(perm_ref[...], value).astype(bf16)

    def stage_c(q):
        def one(s, carry):
            parts = [
                product(fc_ref[s * group + p // b_dev], v_ref[native(s, p), columns(q)]).astype(bf16)
                for p in range(pairs)
            ]
            spread(jnp.concatenate(parts, axis=0), send1, q, s)
            return carry

        lax.fori_loop(0, steps_c, one, 0)
        start(S1, q)

    def stage_g0(q):
        def one(s, carry):
            rows = pl.ds(pl.multiple_of(s * span, 128), span)
            spread(g_ref[rows, columns(q)], send3, q, s)
            return carry

        lax.fori_loop(0, steps_c, one, 0)
        start(S3, q)

    def stage_a(q):
        wait(S1, q, False)

        def one(m, carry):
            value = og[q, m].reshape(outer_rows, width)
            send2[q, m] = product(ma_ref[...], value).astype(bf16).reshape(na, block, width)
            return carry

        lax.fori_loop(0, nb, one, 0)
        start(B1, q)

    def stage_g1(q):
        wait(S3, q, False)
        start(B3, q)

    per_block = block // rows_b

    def middle(ref, q, t):
        rows = pl.ds(pl.multiple_of(lax.rem(t, per_block) * rows_b, 16), rows_b)
        return ref[q, :, lax.div(t, per_block), rows, :].reshape(nb * rows_b, width)

    def put_middle(ref, q, t, value):
        rows = pl.ds(pl.multiple_of(lax.rem(t, per_block) * rows_b, 16), rows_b)
        ref[q, lax.div(t, per_block), :, rows, :] = value.astype(bf16).reshape(nb, rows_b, width)

    def stage_b(q):
        wait(B1, q, False)
        wait(S1, q, True)

        def one(t, carry):
            put_middle(send1, q, t, product(mb_ref[...], middle(ig, q, t)))
            return carry

        lax.fori_loop(0, outer_rows // rows_b, one, 0)
        start(B2, q)

    def stage_g2(q):
        wait(B3, q, False)
        wait(S3, q, True)

        def one(t, carry):
            put_middle(send3, q, t, product_rows(mb_ref[...], middle(gi, q, t)))
            return carry

        lax.fori_loop(0, outer_rows // rows_b, one, 0)
        start(B4, q)

        def gram(t, carry):
            gfb_ref[...] += product_columns(middle(gi, q, t), middle(ig, q, t))
            return carry

        lax.fori_loop(0, outer_rows // rows_b, gram, 0)

    def stage_m1(q):
        wait(B2, q, False)
        start(S2, q)

    def stage_g3(q):
        wait(B4, q, False)
        wait(B1, q, True)

        def one(m, carry):
            grad = g2o[q, m].reshape(outer_rows, width)
            send2[q, m] = product_rows(ma_ref[...], grad).astype(bf16).reshape(na, block, width)
            return carry

        lax.fori_loop(0, nb, one, 0)
        start(S4, q)

        def gram(m, carry):
            gfa_ref[...] += product_columns(
                g2o[q, m].reshape(outer_rows, width), og[q, m].reshape(outer_rows, width)
            )
            return carry

        lax.fori_loop(0, nb, gram, 0)

    def stage_m2(q):
        wait(S2, q, False)

        def one(s, carry):
            rows = pl.ds(pl.multiple_of(s * span, 128), span)
            mix_ref[rows, columns(q)] = unspread(mi, q, s)
            return carry

        lax.fori_loop(0, steps_c, one, 0)

    def stage_g4(q):
        wait(S4, q, False)

        def one(s, carry):
            grad = unspread(g1t, q, s)
            for p in range(pairs):
                part = grad[p * positions : (p + 1) * positions]
                outer = s * group + p // b_dev
                gv_ref[native(s, p), columns(q)] = product_rows(fc_ref[outer], part).astype(bf16)
                gfc_ref[outer] += product_columns(part, v_ref[native(s, p), columns(q)])
            return carry

        lax.fori_loop(0, steps_c, one, 0)

    every = range(chunks)
    for q in every:
        stage_c(q)
    for q in every:
        stage_a(q)
        stage_g0(q)
    for q in every:
        stage_b(q)
        stage_g1(q)
    for q in every:
        stage_g2(q)
        stage_m1(q)
    for q in every:
        stage_m2(q)
    for q in every:
        stage_g3(q)
    for q in every:
        stage_g4(q)
    for q in every:
        for op in (B2, S2, B3, B4, S4):
            wait(op, q, True)


def mixer(na, nb, shape, values, grad_mixing, factor_c, factor_a, factor_b):
    a_dev, b_dev, positions, channels = shape
    bf16, f32 = jnp.bfloat16, jnp.float32
    outer = na * a_dev
    cm = positions // (na * nb)
    rows_c = b_dev * cm
    block = a_dev * rows_c
    group = max(1, 16 // rows_c)
    rows_b = min(block, max(16, 256 // nb))
    share = rows_b // rows_c
    width = 256 if channels % 256 == 0 else channels
    chunks = channels // width
    span = group * b_dev * positions

    def eye(n):
        return jnp.eye(n, dtype=bf16)

    order = jnp.arange(span, dtype=jnp.int32).reshape(group * b_dev, na * nb, cm)
    order = order.transpose(1, 0, 2).reshape(span, 1)
    perm = (order == jnp.arange(span, dtype=jnp.int32)[None, :]).astype(bf16)
    mix_a = (
        factor_a.transpose(1, 0, 2)[:, :, None, :, None, None]
        * eye(b_dev)[None, :, None, None, :, None]
        * eye(cm)[None, None, :, None, None, :]
    ).reshape(outer * rows_c, outer * rows_c)
    wide_b = factor_b.reshape(cm, nb, b_dev, nb, b_dev).transpose(1, 2, 0, 3, 4)
    mix_b = (
        wide_b[:, None, :, :, :, None, :, None]
        * eye(share)[None, :, None, None, None, :, None, None]
        * eye(cm)[None, None, None, :, None, None, None, :]
    ).reshape(nb * rows_b, nb * rows_b)
    dims = (na, nb, a_dev, b_dev, positions, rows_c, group, rows_b, width, chunks)
    by_a = pltpu.VMEM((chunks, na, nb, block, width), bf16)
    by_b = pltpu.VMEM((chunks, nb, na, block, width), bf16)
    vmem = pl.BlockSpec(memory_space=pltpu.VMEM)
    rows = a_dev * b_dev * positions
    mixing, grad_values, gram_c, gram_a, gram_b = pl.pallas_call(
        functools.partial(mixer_kernel, dims),
        out_shape=(
            jax.ShapeDtypeStruct((rows, channels), bf16),
            jax.ShapeDtypeStruct((rows, channels), bf16),
            jax.ShapeDtypeStruct(factor_c.shape, f32),
            jax.ShapeDtypeStruct(mix_a.shape, f32),
            jax.ShapeDtypeStruct(mix_b.shape, f32),
        ),
        in_specs=[vmem] * 6,
        out_specs=(vmem,) * 5,
        scratch_shapes=[
            by_a, by_b, by_a, by_b, by_b, by_b, by_a, by_b, by_b, by_b, by_a,
            pltpu.SemaphoreType.DMA((8, chunks, max(na, nb))),
            pltpu.SemaphoreType.DMA((8, chunks, max(na, nb))),
        ],
        compiler_params=pltpu.CompilerParams(
            collective_id=0, has_side_effects=True, vmem_limit_bytes=62 * 2**20
        ),
        name="mixer",
    )(values, grad_mixing, factor_c, perm, mix_a, mix_b)
    grad_fa = jnp.einsum("kbcabc->bka", gram_a.reshape(outer, b_dev, cm, outer, b_dev, cm))
    grad_fb = jnp.einsum(
        "JgBcjgbc->cJBjb", gram_b.reshape(nb, share, b_dev, cm, nb, share, b_dev, cm)
    ).reshape(factor_b.shape)
    return mixing, grad_values, gram_c, grad_fa, grad_fb


def body(na, nb, tokens, cotangent, in_weight, out_weight, factor_c, factor_a, factor_b):
    a_dev, b_dev, positions, channels = tokens.shape
    row_count = a_dev * b_dev * positions
    grad_scale = 1.0 / math.sqrt(row_count * na * nb)
    flat_tokens = tokens.reshape(row_count, channels)
    projected = jnp.dot(flat_tokens, in_weight, preferred_element_type=jnp.float32)
    queries = projected[:, :channels].astype(jnp.bfloat16)
    values = projected[:, channels:].astype(jnp.bfloat16)
    flat_cotangent = cotangent.reshape(row_count, channels)
    query_wide = queries.astype(jnp.float32)
    sigmoid_q = jax.nn.sigmoid(query_wide)
    activation = query_wide * sigmoid_q
    slope = sigmoid_q * (1.0 + query_wide * (1.0 - sigmoid_q))
    grad_gated = product_columns(flat_cotangent, out_weight)
    grad_mixing = (grad_gated * activation).astype(jnp.bfloat16)
    mixing, grad_values, part_fc, part_fa, grad_fb = mixer(
        na, nb, tokens.shape, values, grad_mixing, factor_c, factor_a, factor_b
    )
    grad_fa = lax.psum(part_fa, "sa")
    grad_fc = lax.psum(part_fc, "sb")
    mixing_wide = mixing.astype(jnp.float32)
    gated = (activation * mixing_wide).astype(jnp.bfloat16)
    grad_queries = (grad_gated * mixing_wide * slope).astype(jnp.bfloat16)
    part_out = product_rows(gated, flat_cotangent)
    grad_projected = jnp.concatenate([grad_queries, grad_values], axis=1)
    grad_tokens = product_columns(grad_projected, in_weight).astype(jnp.bfloat16)
    part_in = product_rows(flat_tokens, grad_projected)
    sum_in, sum_out = lax.psum((part_in, part_out), ("sa", "sb"))
    return (
        grad_tokens.reshape(tokens.shape),
        sum_in * grad_scale,
        sum_out * grad_scale,
        grad_fc * grad_scale,
        grad_fa * grad_scale,
        grad_fb * grad_scale,
    )


def solution(mesh):
    return jax.shard_map(
        functools.partial(body, mesh.shape["sa"], mesh.shape["sb"]),
        mesh=mesh,
        in_specs=(
            P("sa", "sb", None, None),
            P("sa", "sb", None, None),
            P(),
            P(),
            P("sa", None, None),
            P("sb", None, None),
            P(("sa", "sb"), None, None),
        ),
        out_specs=(
            P("sa", "sb", None, None),
            P(),
            P(),
            P("sa", None, None),
            P("sb", None, None),
            P(("sa", "sb"), None, None),
        ),
        check_vma=False,
    )
```

```python
import functools
import math

import jax
import jax.numpy as jnp
from jax import lax
from jax.experimental import pallas as pl
from jax.experimental.pallas import tpu as pltpu
from jax.sharding import PartitionSpec as P

CONTRACT_ROWS = (((0,), (0,)), ((), ()))
CONTRACT_COLUMNS = (((1,), (1,)), ((), ()))
S1, B1, B2, S2, S3, B3, B4, S4 = range(8)


def product_rows(left, right):
    return lax.dot_general(left, right, CONTRACT_ROWS, preferred_element_type=jnp.float32)


def product_columns(left, right):
    return lax.dot_general(left, right, CONTRACT_COLUMNS, preferred_element_type=jnp.float32)


def product(left, right):
    return jnp.dot(left, right, preferred_element_type=jnp.float32)


def mixer_kernel(
    dims,
    v_ref, g_ref, fc_ref, perm_ref, ma_ref, mb_ref,
    mix_ref, gv_ref, gfc_ref, gfa_ref, gfb_ref,
    send1, send2, send3, og, ig, mo, mi, go, gi, g2o, g1t,
    send_sem, recv_sem,
):
    na, nb, a_dev, b_dev, positions, rows_c, group, rows_b, width, chunks = dims
    block = a_dev * rows_c
    outer_rows = na * block
    me_a = lax.axis_index("sa")
    me_b = lax.axis_index("sb")
    bf16 = jnp.bfloat16

    def peer_a(t):
        return lax.rem(me_a + t, na)

    def peer_b(t):
        return lax.rem(me_b + t, nb)

    barrier = pltpu.get_barrier_semaphore()

    def greet_a(t, carry):
        pl.semaphore_signal(barrier, inc=1, device_id={"sa": peer_a(t)}, device_id_type=pl.DeviceIdType.MESH)
        return carry

    def greet_b(t, carry):
        pl.semaphore_signal(barrier, inc=1, device_id={"sb": peer_b(t)}, device_id_type=pl.DeviceIdType.MESH)
        return carry

    lax.fori_loop(1, na, greet_a, 0)
    lax.fori_loop(1, nb, greet_b, 0)
    pl.semaphore_wait(barrier, na + nb - 2)

    gfc_ref[...] = jnp.zeros_like(gfc_ref)
    gfa_ref[...] = jnp.zeros_like(gfa_ref)
    gfb_ref[...] = jnp.zeros_like(gfb_ref)

    def scatter_copy(op, q, src, dst, peer, slot):
        return pltpu.make_async_remote_copy(
            src_ref=src.at[q, peer],
            dst_ref=dst.at[q, :, slot],
            send_sem=send_sem.at[op, q, peer],
            recv_sem=recv_sem.at[op, q, slot],
            device_id={"sa": peer},
            device_id_type=pl.DeviceIdType.MESH,
        )

    def collect_copy(op, q, src, dst, peer, slot):
        return pltpu.make_async_remote_copy(
            src_ref=src.at[q, :, peer],
            dst_ref=dst.at[q, slot],
            send_sem=send_sem.at[op, q, peer],
            recv_sem=recv_sem.at[op, q, slot],
            device_id={"sa": peer},
            device_id_type=pl.DeviceIdType.MESH,
        )

    def middle_copy(op, q, src, dst, peer, slot):
        return pltpu.make_async_remote_copy(
            src_ref=src.at[q, :, peer] if op in (B2, B4) else src.at[q, peer],
            dst_ref=dst.at[q, slot],
            send_sem=send_sem.at[op, q, peer],
            recv_sem=recv_sem.at[op, q, slot],
            device_id={"sb": peer},
            device_id_type=pl.DeviceIdType.MESH,
        )

    plan = {
        S1: (scatter_copy, send1, og),
        S2: (collect_copy, mo, mi),
        S3: (scatter_copy, send3, go),
        S4: (collect_copy, send2, g1t),
        B1: (middle_copy, send2, ig),
        B2: (middle_copy, send1, mo),
        B3: (middle_copy, go, gi),
        B4: (middle_copy, send3, g2o),
    }

    def start(op, q):
        make, src, dst = plan[op]
        over_b = make is middle_copy
        me, size, peer_of = (me_b, nb, peer_b) if over_b else (me_a, na, peer_a)

        def one(t, carry):
            make(op, q, src, dst, peer_of(t), me).start()
            return carry

        lax.fori_loop(1, size, one, 0)
        if make is scatter_copy:
            dst[q, :, me] = src[q, me]
        elif op in (B1, B3):
            dst[q, me] = src[q, me]
        else:
            dst[q, me] = src[q, :, me]

    def wait(op, q, sends):
        make, src, dst = plan[op]
        size, peer_of = (nb, peer_b) if make is middle_copy else (na, peer_a)

        def one(t, carry):
            peer = peer_of(t)
            copy = make(op, q, src, dst, peer, peer)
            if sends:
                copy.wait_send()
            else:
                copy.wait_recv()
            return carry

        lax.fori_loop(1, size, one, 0)

    pairs = group * b_dev
    span = pairs * positions
    steps_c = a_dev // group
    slab = group * rows_c

    def columns(q):
        return slice(q * width, (q + 1) * width)

    def native(s, p):
        return pl.ds(pl.multiple_of(s * span + p * positions, 128), positions)

    def slab_rows(s):
        return pl.ds(pl.multiple_of(s * slab, 16), slab)

    def spread(value, dst, q, s):
        moved = product(perm_ref[...], value).astype(bf16)
        dst[q, :, :, slab_rows(s), :] = moved.reshape(na, nb, slab, width)

    def unspread(src, q, s):
        value = src[q, :, :, slab_rows(s), :].reshape(span, width)
        return product_rows(perm_ref[...], value).astype(bf16)

    def stage_c(q):
        def one(s, carry):
            parts = [
                product(fc_ref[s * group + p // b_dev], v_ref[native(s, p), columns(q)]).astype(bf16)
                for p in range(pairs)
            ]
            spread(jnp.concatenate(parts, axis=0), send1, q, s)
            return carry

        lax.fori_loop(0, steps_c, one, 0)
        start(S1, q)

    def stage_g0(q):
        def one(s, carry):
            rows = pl.ds(pl.multiple_of(s * span, 128), span)
            spread(g_ref[rows, columns(q)], send3, q, s)
            return carry

        lax.fori_loop(0, steps_c, one, 0)
        start(S3, q)

    def stage_a(q):
        wait(S1, q, False)

        def one(m, carry):
            value = og[q, m].reshape(outer_rows, width)
            send2[q, m] = product(ma_ref[...], value).astype(bf16).reshape(na, block, width)
            return carry

        lax.fori_loop(0, nb, one, 0)
        start(B1, q)

    def stage_g1(q):
        wait(S3, q, False)
        start(B3, q)

    per_block = block // rows_b

    def middle(ref, q, t):
        rows = pl.ds(pl.multiple_of(lax.rem(t, per_block) * rows_b, 16), rows_b)
        return ref[q, :, lax.div(t, per_block), rows, :].reshape(nb * rows_b, width)

    def put_middle(ref, q, t, value):
        rows = pl.ds(pl.multiple_of(lax.rem(t, per_block) * rows_b, 16), rows_b)
        ref[q, lax.div(t, per_block), :, rows, :] = value.astype(bf16).reshape(nb, rows_b, width)

    def stage_b(q):
        wait(B1, q, False)
        wait(S1, q, True)

        def one(t, carry):
            put_middle(send1, q, t, product(mb_ref[...], middle(ig, q, t)))
            return carry

        lax.fori_loop(0, outer_rows // rows_b, one, 0)
        start(B2, q)

    def stage_g2(q):
        wait(B3, q, False)
        wait(S3, q, True)

        def one(t, carry):
            put_middle(send3, q, t, product_rows(mb_ref[...], middle(gi, q, t)))
            return carry

        lax.fori_loop(0, outer_rows // rows_b, one, 0)
        start(B4, q)

        def gram(t, carry):
            gfb_ref[...] += product_columns(middle(gi, q, t), middle(ig, q, t))
            return carry

        lax.fori_loop(0, outer_rows // rows_b, gram, 0)

    def stage_m1(q):
        wait(B2, q, False)
        start(S2, q)

    def stage_g3(q):
        wait(B4, q, False)
        wait(B1, q, True)

        def one(m, carry):
            grad = g2o[q, m].reshape(outer_rows, width)
            send2[q, m] = product_rows(ma_ref[...], grad).astype(bf16).reshape(na, block, width)
            return carry

        lax.fori_loop(0, nb, one, 0)
        start(S4, q)

        def gram(m, carry):
            gfa_ref[...] += product_columns(
                g2o[q, m].reshape(outer_rows, width), og[q, m].reshape(outer_rows, width)
            )
            return carry

        lax.fori_loop(0, nb, gram, 0)

    def stage_m2(q):
        wait(S2, q, False)

        def one(s, carry):
            rows = pl.ds(pl.multiple_of(s * span, 128), span)
            mix_ref[rows, columns(q)] = unspread(mi, q, s)
            return carry

        lax.fori_loop(0, steps_c, one, 0)

    def stage_g4(q):
        wait(S4, q, False)

        def one(s, carry):
            grad = unspread(g1t, q, s)
            for p in range(pairs):
                part = grad[p * positions : (p + 1) * positions]
                outer = s * group + p // b_dev
                gv_ref[native(s, p), columns(q)] = product_rows(fc_ref[outer], part).astype(bf16)
                gfc_ref[outer] += product_columns(part, v_ref[native(s, p), columns(q)])
            return carry

        lax.fori_loop(0, steps_c, one, 0)

    every = range(chunks)
    for q in every:
        stage_c(q)
    for q in every:
        stage_a(q)
        stage_g0(q)
    for q in every:
        stage_b(q)
        stage_g1(q)
    for q in every:
        stage_g2(q)
        stage_m1(q)
    for q in every:
        stage_m2(q)
    for q in every:
        stage_g3(q)
    for q in every:
        stage_g4(q)
    for q in every:
        for op in (B2, S2, B3, B4, S4):
            wait(op, q, True)


def mixer(na, nb, shape, values, grad_mixing, factor_c, factor_a, factor_b):
    a_dev, b_dev, positions, channels = shape
    bf16, f32 = jnp.bfloat16, jnp.float32
    outer = na * a_dev
    cm = positions // (na * nb)
    rows_c = b_dev * cm
    block = a_dev * rows_c
    group = max(1, 16 // rows_c)
    rows_b = min(block, max(16, 256 // nb))
    share = rows_b // rows_c
    width = 256 if channels % 256 == 0 else channels
    chunks = channels // width
    span = group * b_dev * positions

    order = jnp.arange(span, dtype=jnp.int32).reshape(group * b_dev, na * nb, cm)
    order = order.transpose(1, 0, 2).reshape(span, 1)
    perm = (order == jnp.arange(span, dtype=jnp.int32)[None, :]).astype(bf16)
    at_a = jnp.arange(outer * rows_c, dtype=jnp.int32)
    same_a = at_a[:, None] % rows_c == at_a[None, :] % rows_c
    wide_a = (jnp.arange(outer, dtype=jnp.int32)[:, None] == at_a[None, :] // rows_c).astype(bf16)
    at_b = jnp.arange(nb * rows_b, dtype=jnp.int32)
    inner_b = at_b // rows_b * b_dev + at_b // cm % b_dev
    kind_b = at_b % rows_b // rows_c * cm + at_b % cm
    same_b = kind_b[:, None] == kind_b[None, :]
    wide_b = (jnp.arange(nb * b_dev, dtype=jnp.int32)[:, None] == inner_b[None, :]).astype(bf16)
    rows_fa = jnp.repeat(factor_a.transpose(1, 0, 2).reshape(outer * b_dev, outer), cm, axis=0)
    mix_a = jnp.where(same_a, product(rows_fa, wide_a), 0.0).astype(bf16)
    rows_fb = factor_b.reshape(cm, nb, 1, b_dev, nb * b_dev).transpose(1, 2, 3, 0, 4)
    rows_fb = jnp.broadcast_to(rows_fb, (nb, share, b_dev, cm, nb * b_dev)).reshape(nb * rows_b, nb * b_dev)
    mix_b = jnp.where(same_b, product(rows_fb, wide_b), 0.0).astype(bf16)
    dims = (na, nb, a_dev, b_dev, positions, rows_c, group, rows_b, width, chunks)
    by_a = pltpu.VMEM((chunks, na, nb, block, width), bf16)
    by_b = pltpu.VMEM((chunks, nb, na, block, width), bf16)
    vmem = pl.BlockSpec(memory_space=pltpu.VMEM)
    rows = a_dev * b_dev * positions
    mixing, grad_values, gram_c, gram_a, gram_b = pl.pallas_call(
        functools.partial(mixer_kernel, dims),
        out_shape=(
            jax.ShapeDtypeStruct((rows, channels), bf16),
            jax.ShapeDtypeStruct((rows, channels), bf16),
            jax.ShapeDtypeStruct(factor_c.shape, f32),
            jax.ShapeDtypeStruct(mix_a.shape, f32),
            jax.ShapeDtypeStruct(mix_b.shape, f32),
        ),
        in_specs=[vmem] * 6,
        out_specs=(vmem,) * 5,
        scratch_shapes=[
            by_a, by_b, by_a, by_b, by_b, by_b, by_a, by_b, by_b, by_b, by_a,
            pltpu.SemaphoreType.DMA((8, chunks, max(na, nb))),
            pltpu.SemaphoreType.DMA((8, chunks, max(na, nb))),
        ],
        compiler_params=pltpu.CompilerParams(
            collective_id=0, has_side_effects=True, vmem_limit_bytes=62 * 2**20
        ),
        name="mixer",
    )(values, grad_mixing, factor_c, perm, mix_a, mix_b)
    def narrow(gram, same, wide):
        return lax.dot_general(
            jnp.where(same, gram, 0.0), wide.astype(f32), CONTRACT_COLUMNS,
            precision=lax.Precision.HIGHEST, preferred_element_type=f32,
        )

    grad_fa = narrow(gram_a, same_a, wide_a).reshape(outer, b_dev, cm, outer).sum(axis=2).transpose(1, 0, 2)
    grad_fb = narrow(gram_b, same_b, wide_b).reshape(nb, share, b_dev, cm, nb * b_dev).sum(axis=1)
    grad_fb = grad_fb.transpose(2, 0, 1, 3).reshape(factor_b.shape)
    return mixing, grad_values, gram_c, grad_fa, grad_fb


def total_kernel(na, nz, chunks, x_ref, out_ref, r0, s0, r1, s1, r2, send_sem, recv_sem):
    me_a = lax.axis_index("sa")
    me_b = lax.axis_index("sb")
    core, me_z = lax.rem(me_b, 2), lax.div(me_b, 2)
    other = 1 - core
    width = x_ref.shape[-1] // chunks
    bf16, f32 = jnp.bfloat16, jnp.float32
    mesh_ids = pl.DeviceIdType.MESH

    def to_a(t):
        return lax.rem(me_a + t, na)

    def to_z(t):
        return lax.rem(me_z + t, nz)

    def on_z(z):
        return {"sb": z * 2 + core}

    barrier = pltpu.get_barrier_semaphore()

    def greet_a(t, carry):
        pl.semaphore_signal(barrier, inc=1, device_id={"sa": to_a(t)}, device_id_type=mesh_ids)
        return carry

    def greet_z(t, carry):
        pl.semaphore_signal(barrier, inc=1, device_id=on_z(to_z(t)), device_id_type=mesh_ids)
        return carry

    lax.fori_loop(1, na, greet_a, 0)
    lax.fori_loop(1, nz, greet_z, 0)
    pl.semaphore_signal(barrier, inc=1, device_id={"sb": me_z * 2 + other}, device_id_type=mesh_ids)
    pl.semaphore_wait(barrier, na + nz - 1)

    def columns(q):
        return slice(q * width, (q + 1) * width)

    def copy(stage, q, peer, slot):
        cols = columns(q)
        if stage == 0:
            src, dst, target = x_ref.at[other, :, :, :, cols], r0.at[q], {"sb": me_z * 2 + other}
        elif stage == 1:
            src, dst, target = s0.at[q, peer], r1.at[q, slot], {"sa": peer}
        elif stage == 2:
            src, dst, target = s1.at[q, peer], r2.at[q, slot], on_z(peer)
        elif stage == 3:
            src, dst = out_ref.at[core, me_a, me_z, :, cols], out_ref.at[core, me_a, slot, :, cols]
            target = on_z(peer)
        elif stage == 4:
            src, dst = out_ref.at[core, me_a, :, :, cols], out_ref.at[core, slot, :, :, cols]
            target = {"sa": peer}
        else:
            src, dst = out_ref.at[core, :, :, :, cols], out_ref.at[slot, :, :, :, cols]
            target = {"sb": me_z * 2 + other}
        return pltpu.make_async_remote_copy(
            src_ref=src, dst_ref=dst, send_sem=send_sem.at[stage, q, peer], recv_sem=recv_sem.at[stage, q, slot],
            device_id=target, device_id_type=mesh_ids,
        )

    def each(stage, act):
        if stage in (0, 5):
            act(other, core)
            return
        size, peer_of, me = (na, to_a, me_a) if stage in (1, 4) else (nz, to_z, me_z)

        def one(t, carry):
            act(peer_of(t), me)
            return carry

        lax.fori_loop(1, size, one, 0)

    def start(stage, q):
        each(stage, lambda peer, me: copy(stage, q, peer, me).start())

    def arrive(stage, q):
        each(stage, lambda peer, me: copy(stage, q, peer, peer).wait_recv())

    every = range(chunks)
    for q in every:
        start(0, q)
    for q in every:
        arrive(0, q)

        def pair(i, carry):
            s0[q, i] = (x_ref[core, i, :, :, columns(q)].astype(f32) + r0[q, i].astype(f32)).astype(bf16)
            return carry

        lax.fori_loop(0, na, pair, 0)
        start(1, q)
    for q in every:
        arrive(1, q)

        def across(z, carry):
            total = s0[q, me_a, z].astype(f32)
            for t in range(1, na):
                total += r1[q, to_a(t), z].astype(f32)
            s1[q, z] = total.astype(bf16)
            return carry

        lax.fori_loop(0, nz, across, 0)
        start(2, q)
    for q in every:
        arrive(2, q)
        total = s1[q, me_z].astype(f32)
        for t in range(1, nz):
            total += r2[q, to_z(t)].astype(f32)
        out_ref[core, me_a, me_z, :, columns(q)] = total.astype(bf16)
        start(3, q)
    for q in every:
        arrive(3, q)
        start(4, q)
    for q in every:
        arrive(4, q)
        start(5, q)
    for q in every:
        arrive(5, q)
    for q in every:
        for stage in range(6):
            each(stage, lambda peer, me: copy(stage, q, peer, me).wait_send())


def total(na, nb, parts):
    nz = nb // 2
    rows, channels = sum(part.shape[0] for part in parts), parts[0].shape[1]
    share = -(-rows // (na * nb * 16)) * 16
    filler = jnp.zeros((share * na * nb - rows, channels), jnp.bfloat16)
    stacked = jnp.concatenate([*parts, filler], axis=0).reshape(2, na, nz, share, channels)
    chunks = channels // 256 if channels % 256 == 0 else 1
    width = channels // chunks
    vmem = pl.BlockSpec(memory_space=pltpu.VMEM)
    by_a = pltpu.VMEM((chunks, na, nz, share, width), jnp.bfloat16)
    by_z = pltpu.VMEM((chunks, nz, share, width), jnp.bfloat16)
    sems = pltpu.SemaphoreType.DMA((6, chunks, max(na, nz, 2)))
    summed = pl.pallas_call(
        functools.partial(total_kernel, na, nz, chunks),
        out_shape=jax.ShapeDtypeStruct(stacked.shape, jnp.bfloat16),
        in_specs=[vmem],
        out_specs=vmem,
        scratch_shapes=[by_a, by_a, by_a, by_z, by_z, sems, sems],
        compiler_params=pltpu.CompilerParams(
            collective_id=1, has_side_effects=True, vmem_limit_bytes=48 * 2**20
        ),
        name="total",
    )(stacked).reshape(share * na * nb, channels)
    ends, begin = [], 0
    for part in parts:
        ends.append(summed[begin : begin + part.shape[0]].astype(jnp.float32))
        begin += part.shape[0]
    return ends

def body(na, nb, tokens, cotangent, in_weight, out_weight, factor_c, factor_a, factor_b):
    a_dev, b_dev, positions, channels = tokens.shape
    row_count = a_dev * b_dev * positions
    grad_scale = 1.0 / math.sqrt(row_count * na * nb)
    flat_tokens = tokens.reshape(row_count, channels)
    projected = jnp.dot(flat_tokens, in_weight, preferred_element_type=jnp.float32)
    queries = projected[:, :channels].astype(jnp.bfloat16)
    values = projected[:, channels:].astype(jnp.bfloat16)
    flat_cotangent = cotangent.reshape(row_count, channels)
    query_wide = queries.astype(jnp.float32)
    sigmoid_q = jax.nn.sigmoid(query_wide)
    activation = query_wide * sigmoid_q
    slope = sigmoid_q * (1.0 + query_wide * (1.0 - sigmoid_q))
    grad_gated = product_columns(flat_cotangent, out_weight)
    grad_mixing = (grad_gated * activation).astype(jnp.bfloat16)
    mixing, grad_values, part_fc, part_fa, grad_fb = mixer(
        na, nb, tokens.shape, values, grad_mixing, factor_c, factor_a, factor_b
    )
    grad_fa = lax.psum(part_fa, "sa")
    grad_fc = lax.psum(part_fc, "sb")
    mixing_wide = mixing.astype(jnp.float32)
    gated = (activation * mixing_wide).astype(jnp.bfloat16)
    grad_queries = (grad_gated * mixing_wide * slope).astype(jnp.bfloat16)
    part_out = product_rows(gated, flat_cotangent).astype(jnp.bfloat16)
    part_queries = product_rows(flat_tokens, grad_queries).astype(jnp.bfloat16)
    part_values = product_rows(flat_tokens, grad_values).astype(jnp.bfloat16)
    grad_projected = jnp.concatenate([grad_queries, grad_values], axis=1)
    grad_tokens = product_columns(grad_projected, in_weight).astype(jnp.bfloat16)
    sum_out, sum_queries, sum_values = total(na, nb, (part_out, part_queries, part_values))
    sum_in = jnp.concatenate([sum_queries, sum_values], axis=1)
    return (
        grad_tokens.reshape(tokens.shape),
        sum_in * grad_scale,
        sum_out * grad_scale,
        grad_fc * grad_scale,
        grad_fa * grad_scale,
        grad_fb * grad_scale,
    )


def solution(mesh):
    return jax.shard_map(
        functools.partial(body, mesh.shape["sa"], mesh.shape["sb"]),
        mesh=mesh,
        in_specs=(
            P("sa", "sb", None, None),
            P("sa", "sb", None, None),
            P(),
            P(),
            P("sa", None, None),
            P("sb", None, None),
            P(("sa", "sb"), None, None),
        ),
        out_specs=(
            P("sa", "sb", None, None),
            P(),
            P(),
            P("sa", None, None),
            P("sb", None, None),
            P(("sa", "sb"), None, None),
        ),
        check_vma=False,
    )
```

```python
import functools
import math

import jax
import jax.numpy as jnp
from jax import lax
from jax.experimental import pallas as pl
from jax.experimental.pallas import tpu as pltpu
from jax.sharding import PartitionSpec as P

CONTRACT_ROWS = (((0,), (0,)), ((), ()))
CONTRACT_COLUMNS = (((1,), (1,)), ((), ()))
S1, B1, B2, S2, S3, B3, B4, S4 = range(8)


def product_rows(left, right):
    return lax.dot_general(left, right, CONTRACT_ROWS, preferred_element_type=jnp.float32)


def product_columns(left, right):
    return lax.dot_general(left, right, CONTRACT_COLUMNS, preferred_element_type=jnp.float32)


def product(left, right):
    return jnp.dot(left, right, preferred_element_type=jnp.float32)


def mixer_kernel(
    dims,
    v_ref, g_ref, fc_ref, perm_ref, ma_ref, mb_ref,
    mix_ref, gv_ref, gfc_ref, gfa_ref, gfb_ref,
    send1, send2, send3, og, ig, mo, mi, go, gi, g2o, g1t,
    send_sem, recv_sem,
):
    na, nb, a_dev, b_dev, positions, rows_c, group, rows_b, width, chunks = dims
    block = a_dev * rows_c
    outer_rows = na * block
    me_a = lax.axis_index("sa")
    me_b = lax.axis_index("sb")
    bf16 = jnp.bfloat16

    def peer_a(t):
        return lax.rem(me_a + t, na)

    def peer_b(t):
        return lax.rem(me_b + t, nb)

    barrier = pltpu.get_barrier_semaphore()

    def greet_a(t, carry):
        pl.semaphore_signal(barrier, inc=1, device_id={"sa": peer_a(t)}, device_id_type=pl.DeviceIdType.MESH)
        return carry

    def greet_b(t, carry):
        pl.semaphore_signal(barrier, inc=1, device_id={"sb": peer_b(t)}, device_id_type=pl.DeviceIdType.MESH)
        return carry

    lax.fori_loop(1, na, greet_a, 0)
    lax.fori_loop(1, nb, greet_b, 0)
    pl.semaphore_wait(barrier, na + nb - 2)

    gfc_ref[...] = jnp.zeros_like(gfc_ref)
    gfa_ref[...] = jnp.zeros_like(gfa_ref)
    gfb_ref[...] = jnp.zeros_like(gfb_ref)

    def scatter_copy(op, q, src, dst, peer, slot):
        return pltpu.make_async_remote_copy(
            src_ref=src.at[q, peer],
            dst_ref=dst.at[q, :, slot],
            send_sem=send_sem.at[op, q, peer],
            recv_sem=recv_sem.at[op, q, slot],
            device_id={"sa": peer},
            device_id_type=pl.DeviceIdType.MESH,
        )

    def collect_copy(op, q, src, dst, peer, slot):
        return pltpu.make_async_remote_copy(
            src_ref=src.at[q, :, peer],
            dst_ref=dst.at[q, slot],
            send_sem=send_sem.at[op, q, peer],
            recv_sem=recv_sem.at[op, q, slot],
            device_id={"sa": peer},
            device_id_type=pl.DeviceIdType.MESH,
        )

    def middle_copy(op, q, src, dst, peer, slot):
        return pltpu.make_async_remote_copy(
            src_ref=src.at[q, :, peer] if op in (B2, B4) else src.at[q, peer],
            dst_ref=dst.at[q, slot],
            send_sem=send_sem.at[op, q, peer],
            recv_sem=recv_sem.at[op, q, slot],
            device_id={"sb": peer},
            device_id_type=pl.DeviceIdType.MESH,
        )

    plan = {
        S1: (scatter_copy, send1, og),
        S2: (collect_copy, mo, mi),
        S3: (scatter_copy, send3, go),
        S4: (collect_copy, send2, g1t),
        B1: (middle_copy, send2, ig),
        B2: (middle_copy, send1, mo),
        B3: (middle_copy, go, gi),
        B4: (middle_copy, send3, g2o),
    }

    def start(op, q):
        make, src, dst = plan[op]
        over_b = make is middle_copy
        me, size, peer_of = (me_b, nb, peer_b) if over_b else (me_a, na, peer_a)

        def one(t, carry):
            make(op, q, src, dst, peer_of(t), me).start()
            return carry

        lax.fori_loop(1, size, one, 0)
        if make is scatter_copy:
            dst[q, :, me] = src[q, me]
        elif op in (B1, B3):
            dst[q, me] = src[q, me]
        else:
            dst[q, me] = src[q, :, me]

    def wait(op, q, sends):
        make, src, dst = plan[op]
        size, peer_of = (nb, peer_b) if make is middle_copy else (na, peer_a)

        def one(t, carry):
            peer = peer_of(t)
            copy = make(op, q, src, dst, peer, peer)
            if sends:
                copy.wait_send()
            else:
                copy.wait_recv()
            return carry

        lax.fori_loop(1, size, one, 0)

    pairs = group * b_dev
    span = pairs * positions
    steps_c = a_dev // group
    slab = group * rows_c

    def columns(q):
        return slice(q * width, (q + 1) * width)

    def native(s, p):
        return pl.ds(pl.multiple_of(s * span + p * positions, 128), positions)

    def slab_rows(s):
        return pl.ds(pl.multiple_of(s * slab, 16), slab)

    def spread(value, dst, q, s):
        moved = product(perm_ref[...], value).astype(bf16)
        dst[q, :, :, slab_rows(s), :] = moved.reshape(na, nb, slab, width)

    def unspread(src, q, s):
        value = src[q, :, :, slab_rows(s), :].reshape(span, width)
        return product_rows(perm_ref[...], value).astype(bf16)

    def stage_c(q):
        def one(s, carry):
            parts = [
                product(fc_ref[s * group + p // b_dev], v_ref[native(s, p), columns(q)]).astype(bf16)
                for p in range(pairs)
            ]
            spread(jnp.concatenate(parts, axis=0), send1, q, s)
            return carry

        lax.fori_loop(0, steps_c, one, 0)
        start(S1, q)

    def stage_g0(q):
        def one(s, carry):
            rows = pl.ds(pl.multiple_of(s * span, 128), span)
            spread(g_ref[rows, columns(q)], send3, q, s)
            return carry

        lax.fori_loop(0, steps_c, one, 0)
        start(S3, q)

    def stage_a(q):
        wait(S1, q, False)

        def one(m, carry):
            value = og[q, m].reshape(outer_rows, width)
            send2[q, m] = product(ma_ref[...], value).astype(bf16).reshape(na, block, width)
            return carry

        lax.fori_loop(0, nb, one, 0)
        start(B1, q)

    def stage_g1(q):
        wait(S3, q, False)
        start(B3, q)

    per_block = block // rows_b

    def middle(ref, q, t):
        rows = pl.ds(pl.multiple_of(lax.rem(t, per_block) * rows_b, 16), rows_b)
        return ref[q, :, lax.div(t, per_block), rows, :].reshape(nb * rows_b, width)

    def put_middle(ref, q, t, value):
        rows = pl.ds(pl.multiple_of(lax.rem(t, per_block) * rows_b, 16), rows_b)
        ref[q, lax.div(t, per_block), :, rows, :] = value.astype(bf16).reshape(nb, rows_b, width)

    def stage_b(q):
        wait(B1, q, False)
        wait(S1, q, True)

        def one(t, carry):
            put_middle(send1, q, t, product(mb_ref[...], middle(ig, q, t)))
            return carry

        lax.fori_loop(0, outer_rows // rows_b, one, 0)
        start(B2, q)

    def stage_g2(q):
        wait(B3, q, False)
        wait(S3, q, True)

        def one(t, carry):
            put_middle(send3, q, t, product_rows(mb_ref[...], middle(gi, q, t)))
            return carry

        lax.fori_loop(0, outer_rows // rows_b, one, 0)
        start(B4, q)

        def gram(t, carry):
            gfb_ref[...] += product_columns(middle(gi, q, t), middle(ig, q, t))
            return carry

        lax.fori_loop(0, outer_rows // rows_b, gram, 0)

    def stage_m1(q):
        wait(B2, q, False)
        start(S2, q)

    def stage_g3(q):
        wait(B4, q, False)
        wait(B1, q, True)

        def one(m, carry):
            grad = g2o[q, m].reshape(outer_rows, width)
            send2[q, m] = product_rows(ma_ref[...], grad).astype(bf16).reshape(na, block, width)
            return carry

        lax.fori_loop(0, nb, one, 0)
        start(S4, q)

        def gram(m, carry):
            gfa_ref[...] += product_columns(
                g2o[q, m].reshape(outer_rows, width), og[q, m].reshape(outer_rows, width)
            )
            return carry

        lax.fori_loop(0, nb, gram, 0)

    def stage_m2(q):
        wait(S2, q, False)

        def one(s, carry):
            rows = pl.ds(pl.multiple_of(s * span, 128), span)
            mix_ref[rows, columns(q)] = unspread(mi, q, s)
            return carry

        lax.fori_loop(0, steps_c, one, 0)

    def stage_g4(q):
        wait(S4, q, False)

        def one(s, carry):
            grad = unspread(g1t, q, s)
            for p in range(pairs):
                part = grad[p * positions : (p + 1) * positions]
                outer = s * group + p // b_dev
                gv_ref[native(s, p), columns(q)] = product_rows(fc_ref[outer], part).astype(bf16)
                gfc_ref[outer] += product_columns(part, v_ref[native(s, p), columns(q)])
            return carry

        lax.fori_loop(0, steps_c, one, 0)

    every = range(chunks)
    for q in every:
        stage_c(q)
    for q in every:
        stage_a(q)
        stage_g0(q)
    for q in every:
        stage_b(q)
        stage_g1(q)
    for q in every:
        stage_g2(q)
        stage_m1(q)
    for q in every:
        stage_m2(q)
    for q in every:
        stage_g3(q)
    for q in every:
        stage_g4(q)
    for q in every:
        for op in (B2, S2, B3, B4, S4):
            wait(op, q, True)


def mixer(na, nb, shape, values, grad_mixing, factor_c, factor_a, factor_b):
    a_dev, b_dev, positions, channels = shape
    bf16, f32 = jnp.bfloat16, jnp.float32
    outer = na * a_dev
    cm = positions // (na * nb)
    rows_c = b_dev * cm
    block = a_dev * rows_c
    group = max(1, 16 // rows_c)
    rows_b = min(block, max(16, 256 // nb))
    share = rows_b // rows_c
    width = 256 if channels % 256 == 0 else channels
    chunks = channels // width
    span = group * b_dev * positions

    order = jnp.arange(span, dtype=jnp.int32).reshape(group * b_dev, na * nb, cm)
    order = order.transpose(1, 0, 2).reshape(span, 1)
    perm = (order == jnp.arange(span, dtype=jnp.int32)[None, :]).astype(bf16)
    at_a = jnp.arange(outer * rows_c, dtype=jnp.int32)
    same_a = at_a[:, None] % rows_c == at_a[None, :] % rows_c
    wide_a = (jnp.arange(outer, dtype=jnp.int32)[:, None] == at_a[None, :] // rows_c).astype(bf16)
    at_b = jnp.arange(nb * rows_b, dtype=jnp.int32)
    inner_b = at_b // rows_b * b_dev + at_b // cm % b_dev
    kind_b = at_b % rows_b // rows_c * cm + at_b % cm
    same_b = kind_b[:, None] == kind_b[None, :]
    wide_b = (jnp.arange(nb * b_dev, dtype=jnp.int32)[:, None] == inner_b[None, :]).astype(bf16)
    rows_fa = jnp.repeat(factor_a.transpose(1, 0, 2).reshape(outer * b_dev, outer), cm, axis=0)
    mix_a = jnp.where(same_a, product(rows_fa, wide_a), 0.0).astype(bf16)
    rows_fb = factor_b.reshape(cm, nb, 1, b_dev, nb * b_dev).transpose(1, 2, 3, 0, 4)
    rows_fb = jnp.broadcast_to(rows_fb, (nb, share, b_dev, cm, nb * b_dev)).reshape(nb * rows_b, nb * b_dev)
    mix_b = jnp.where(same_b, product(rows_fb, wide_b), 0.0).astype(bf16)
    dims = (na, nb, a_dev, b_dev, positions, rows_c, group, rows_b, width, chunks)
    by_a = pltpu.VMEM((chunks, na, nb, block, width), bf16)
    by_b = pltpu.VMEM((chunks, nb, na, block, width), bf16)
    vmem = pl.BlockSpec(memory_space=pltpu.VMEM)
    rows = a_dev * b_dev * positions
    mixing, grad_values, gram_c, gram_a, gram_b = pl.pallas_call(
        functools.partial(mixer_kernel, dims),
        out_shape=(
            jax.ShapeDtypeStruct((rows, channels), bf16),
            jax.ShapeDtypeStruct((rows, channels), bf16),
            jax.ShapeDtypeStruct(factor_c.shape, f32),
            jax.ShapeDtypeStruct(mix_a.shape, f32),
            jax.ShapeDtypeStruct(mix_b.shape, f32),
        ),
        in_specs=[vmem] * 6,
        out_specs=(vmem,) * 5,
        scratch_shapes=[
            by_a, by_b, by_a, by_b, by_b, by_b, by_a, by_b, by_b, by_b, by_a,
            pltpu.SemaphoreType.DMA((8, chunks, max(na, nb))),
            pltpu.SemaphoreType.DMA((8, chunks, max(na, nb))),
        ],
        compiler_params=pltpu.CompilerParams(
            collective_id=0, has_side_effects=True, vmem_limit_bytes=62 * 2**20
        ),
        name="mixer",
    )(values, grad_mixing, factor_c, perm, mix_a, mix_b)
    def narrow(gram, same, wide):
        return lax.dot_general(
            jnp.where(same, gram, 0.0), wide.astype(f32), CONTRACT_COLUMNS,
            precision=lax.Precision.HIGHEST, preferred_element_type=f32,
        )

    grad_fa = narrow(gram_a, same_a, wide_a).reshape(outer, b_dev, cm, outer).sum(axis=2).transpose(1, 0, 2)
    grad_fb = narrow(gram_b, same_b, wide_b).reshape(nb, share, b_dev, cm, nb * b_dev).sum(axis=1)
    grad_fb = grad_fb.transpose(2, 0, 1, 3).reshape(factor_b.shape)
    return mixing, grad_values, gram_c, grad_fa, grad_fb


def total_kernel(na, nz, chunks, x_ref, out_ref, r0, s0, r1, s1, r2, send_sem, recv_sem):
    me_a = lax.axis_index("sa")
    me_b = lax.axis_index("sb")
    core, me_z = lax.rem(me_b, 2), lax.div(me_b, 2)
    other = 1 - core
    width = x_ref.shape[-1] // chunks
    bf16, f32 = jnp.bfloat16, jnp.float32
    mesh_ids = pl.DeviceIdType.MESH

    def to_a(t):
        return lax.rem(me_a + t, na)

    def to_z(t):
        return lax.rem(me_z + t, nz)

    def on_z(z):
        return {"sb": z * 2 + core}

    barrier = pltpu.get_barrier_semaphore()

    def greet_a(t, carry):
        pl.semaphore_signal(barrier, inc=1, device_id={"sa": to_a(t)}, device_id_type=mesh_ids)
        return carry

    def greet_z(t, carry):
        pl.semaphore_signal(barrier, inc=1, device_id=on_z(to_z(t)), device_id_type=mesh_ids)
        return carry

    lax.fori_loop(1, na, greet_a, 0)
    lax.fori_loop(1, nz, greet_z, 0)
    pl.semaphore_signal(barrier, inc=1, device_id={"sb": me_z * 2 + other}, device_id_type=mesh_ids)
    pl.semaphore_wait(barrier, na + nz - 1)

    def columns(q):
        return slice(q * width, (q + 1) * width)

    def copy(stage, q, peer, slot):
        cols = columns(q)
        if stage == 0:
            src, dst, target = x_ref.at[other, :, :, :, cols], r0.at[q], {"sb": me_z * 2 + other}
        elif stage == 1:
            src, dst, target = s0.at[q, peer], r1.at[q, slot], {"sa": peer}
        elif stage == 2:
            src, dst, target = s1.at[q, peer], r2.at[q, slot], on_z(peer)
        elif stage == 3:
            src, dst = out_ref.at[core, me_a, me_z, :, cols], out_ref.at[core, me_a, slot, :, cols]
            target = on_z(peer)
        elif stage == 4:
            src, dst = out_ref.at[core, me_a, :, :, cols], out_ref.at[core, slot, :, :, cols]
            target = {"sa": peer}
        else:
            src, dst = out_ref.at[core, :, :, :, cols], out_ref.at[slot, :, :, :, cols]
            target = {"sb": me_z * 2 + other}
        return pltpu.make_async_remote_copy(
            src_ref=src, dst_ref=dst, send_sem=send_sem.at[stage, q, peer], recv_sem=recv_sem.at[stage, q, slot],
            device_id=target, device_id_type=mesh_ids,
        )

    def each(stage, act):
        if stage in (0, 5):
            act(other, core)
            return
        size, peer_of, me = (na, to_a, me_a) if stage in (1, 4) else (nz, to_z, me_z)

        def one(t, carry):
            act(peer_of(t), me)
            return carry

        lax.fori_loop(1, size, one, 0)

    def start(stage, q):
        each(stage, lambda peer, me: copy(stage, q, peer, me).start())

    def arrive(stage, q):
        each(stage, lambda peer, me: copy(stage, q, peer, peer).wait_recv())

    every = range(chunks)
    for q in every:
        start(0, q)
    for q in every:
        arrive(0, q)

        def pair(i, carry):
            s0[q, i] = (x_ref[core, i, :, :, columns(q)].astype(f32) + r0[q, i].astype(f32)).astype(bf16)
            return carry

        lax.fori_loop(0, na, pair, 0)
        start(1, q)
    for q in every:
        arrive(1, q)

        def across(z, carry):
            total = s0[q, me_a, z].astype(f32)
            for t in range(1, na):
                total += r1[q, to_a(t), z].astype(f32)
            s1[q, z] = total.astype(bf16)
            return carry

        lax.fori_loop(0, nz, across, 0)
        start(2, q)
    for q in every:
        arrive(2, q)
        total = s1[q, me_z].astype(f32)
        for t in range(1, nz):
            total += r2[q, to_z(t)].astype(f32)
        out_ref[core, me_a, me_z, :, columns(q)] = total.astype(bf16)
        start(3, q)
    for q in every:
        arrive(3, q)
        start(4, q)
    for q in every:
        arrive(4, q)
        start(5, q)
    for q in every:
        arrive(5, q)
    for q in every:
        for stage in range(6):
            each(stage, lambda peer, me: copy(stage, q, peer, me).wait_send())


def total(na, nb, parts):
    nz = nb // 2
    rows, channels = sum(part.shape[0] for part in parts), parts[0].shape[1]
    share = -(-rows // (na * nb * 16)) * 16
    filler = jnp.zeros((share * na * nb - rows, channels), jnp.bfloat16)
    stacked = jnp.concatenate([*parts, filler], axis=0).reshape(2, na, nz, share, channels)
    chunks = channels // 256 if channels % 256 == 0 else 1
    width = channels // chunks
    vmem = pl.BlockSpec(memory_space=pltpu.VMEM)
    by_a = pltpu.VMEM((chunks, na, nz, share, width), jnp.bfloat16)
    by_z = pltpu.VMEM((chunks, nz, share, width), jnp.bfloat16)
    sems = pltpu.SemaphoreType.DMA((6, chunks, max(na, nz, 2)))
    summed = pl.pallas_call(
        functools.partial(total_kernel, na, nz, chunks),
        out_shape=jax.ShapeDtypeStruct(stacked.shape, jnp.bfloat16),
        in_specs=[vmem],
        out_specs=vmem,
        scratch_shapes=[by_a, by_a, by_a, by_z, by_z, sems, sems],
        compiler_params=pltpu.CompilerParams(
            collective_id=1, has_side_effects=True, vmem_limit_bytes=48 * 2**20
        ),
        name="total",
    )(stacked).reshape(share * na * nb, channels)
    ends, begin = [], 0
    for part in parts:
        ends.append(summed[begin : begin + part.shape[0]].astype(jnp.float32))
        begin += part.shape[0]
    return ends

def body(na, nb, tokens, cotangent, in_weight, out_weight, factor_c, factor_a, factor_b):
    a_dev, b_dev, positions, channels = tokens.shape
    row_count = a_dev * b_dev * positions
    grad_scale = 1.0 / math.sqrt(row_count * na * nb)
    flat_tokens = tokens.reshape(row_count, channels)
    projected = jnp.dot(flat_tokens, in_weight, preferred_element_type=jnp.float32)
    queries = projected[:, :channels].astype(jnp.bfloat16)
    values = projected[:, channels:].astype(jnp.bfloat16)
    flat_cotangent = cotangent.reshape(row_count, channels)
    query_wide = queries.astype(jnp.float32)
    sigmoid_q = jax.nn.sigmoid(query_wide)
    activation = query_wide * sigmoid_q
    slope = sigmoid_q * (1.0 + query_wide * (1.0 - sigmoid_q))
    grad_gated = product_columns(flat_cotangent, out_weight)
    grad_mixing = (grad_gated * activation).astype(jnp.bfloat16)
    mixing, grad_values, part_fc, part_fa, grad_fb = mixer(
        na, nb, tokens.shape, values, grad_mixing, factor_c, factor_a, factor_b
    )
    me_b = lax.axis_index("sb")
    fa_rows = -(-part_fa.size // channels)
    flat_fa = jnp.pad(part_fa.reshape(-1), (0, fa_rows * channels - part_fa.size)).reshape(1, fa_rows, channels)
    mine = (jnp.arange(nb, dtype=jnp.int32) == me_b)[:, None, None]
    placed_fa = jnp.where(mine, flat_fa, 0.0).astype(jnp.bfloat16).reshape(nb * fa_rows, channels)
    grad_fc = lax.psum(part_fc, "sb")
    mixing_wide = mixing.astype(jnp.float32)
    gated = (activation * mixing_wide).astype(jnp.bfloat16)
    grad_queries = (grad_gated * mixing_wide * slope).astype(jnp.bfloat16)
    part_out = product_rows(gated, flat_cotangent).astype(jnp.bfloat16)
    part_queries = product_rows(flat_tokens, grad_queries).astype(jnp.bfloat16)
    part_values = product_rows(flat_tokens, grad_values).astype(jnp.bfloat16)
    grad_projected = jnp.concatenate([grad_queries, grad_values], axis=1)
    grad_tokens = product_columns(grad_projected, in_weight).astype(jnp.bfloat16)
    sum_out, sum_queries, sum_values, sum_fa = total(na, nb, (part_out, part_queries, part_values, placed_fa))
    grad_fa = lax.dynamic_slice_in_dim(sum_fa, me_b * fa_rows, fa_rows)
    grad_fa = grad_fa.reshape(-1)[: part_fa.size].reshape(part_fa.shape)
    sum_in = jnp.concatenate([sum_queries, sum_values], axis=1)
    return (
        grad_tokens.reshape(tokens.shape),
        sum_in * grad_scale,
        sum_out * grad_scale,
        grad_fc * grad_scale,
        grad_fa * grad_scale,
        grad_fb * grad_scale,
    )


def solution(mesh):
    return jax.shard_map(
        functools.partial(body, mesh.shape["sa"], mesh.shape["sb"]),
        mesh=mesh,
        in_specs=(
            P("sa", "sb", None, None),
            P("sa", "sb", None, None),
            P(),
            P(),
            P("sa", None, None),
            P("sb", None, None),
            P(("sa", "sb"), None, None),
        ),
        out_specs=(
            P("sa", "sb", None, None),
            P(),
            P(),
            P("sa", None, None),
            P("sb", None, None),
            P(("sa", "sb"), None, None),
        ),
        check_vma=False,
    )
```
